32 devices in a mesh: row: 4 (over x, core), col: 8 (over z, y).
Axes of the slice: x: 2, y: 2, z: 4, core: 2. Of those that a mesh axis runs over, the one named last changes fastest.
Arguments:
- pair: bfloat16 [768, 768, 128], P('row', 'col'), may hold values from -6 to 6
- ln_gain: float32 [128], replicated, may hold values from 0.25 to 1.75
- w_query: bfloat16 [128, 128], replicated, may hold values from -46 to 46
- w_key: bfloat16 [128, 128], replicated, may hold values from -0.5 to 0.5
- w_value: bfloat16 [128, 128], replicated, may hold values from -0.5 to 0.5
- w_gate: bfloat16 [128, 128], replicated, may hold values from -0.5 to 0.5
- w_bias: bfloat16 [128, 4], replicated, may hold values from -0.5 to 0.5
- w_out: bfloat16 [128, 128], replicated, may hold values from -0.5 to 0.5
- valid_length: int32 [1], replicated, may hold values from 384 to 768
Outputs:
- update: bfloat16 [768, 768, 128], P('row', 'col')
The draws below stay inside these ranges and needn't reach their ends.
Inputs may be any that keep to these rules, and one draw needn't show every extreme that they name: Tokens 0 to valid_length - 1 are real, the others are padding.
All inputs are finite; a program needn't handle non-finite values.
Results may differ from the reference program's by a relative error of at most 0.014.
The reference program's roundings to bfloat16 on the way count: a program that leaves them out, or rounds other values in their place, can miss the bound.
Values may be sent and summed in bfloat16 or wider, within the bound.
A program may use at most 384 MiB of HBM per device.

```python
import math
import jax
import jax.numpy as jnp
from jax import lax

C = 128
H = 4
DH = 32
N = 768


def draw_w_query(key, part):
    sample = jnp.clip(jax.random.normal(key, (C, H * DH), jnp.float32), -4.0, 4.0) / math.sqrt(C)
    return sample.astype(jnp.bfloat16)


def steps_of(rng, shape, cuts, low, high):
    gain, own = 1.0, jax.random.fold_in(rng, 6)
    for dim, parts in cuts:
        heights = jnp.exp(jax.random.uniform(jax.random.fold_in(own, dim), (parts,), jnp.float32, low / len(cuts), high / len(cuts)))
        gain = gain * jnp.repeat(heights, shape[dim] // parts).reshape([-1 if axis == dim else 1 for axis in range(len(shape))])
    return gain


def normal_values(stream_key, dims, deviation, limit, cuts=(), kind=jnp.bfloat16):
    result = jax.random.normal(stream_key, dims, jnp.float32) * deviation
    if len(cuts) > 0:
        result = steps_of(stream_key, dims, cuts, -0.22, 0.18) * result
    return jnp.clip(result, min=-limit, max=limit).astype(kind)


def setup_inputs(seed: int = 0) -> dict:
    arg_keys = jax.random.split(jax.random.key(seed), 10)
    return {
        "pair": normal_values(arg_keys[0], (N, N, C), 1.0, 6.0, ((0, 4), (1, 8))),
        "ln_gain": jnp.clip(1.0 + 0.15 * jax.random.normal(arg_keys[1], (C,), jnp.float32), 0.25, 1.75),
        "w_query": draw_w_query(jax.random.fold_in(arg_keys[9], 71), 0),
        "w_key": normal_values(arg_keys[3], (C, H * DH), C ** -0.5, 0.5),
        "w_value": normal_values(arg_keys[4], (C, H * DH), C ** -0.5, 0.5),
        "w_gate": normal_values(arg_keys[5], (C, H * DH), C ** -0.5, 0.5),
        "w_bias": normal_values(arg_keys[6], (C, H), C ** -0.5, 0.5),
        "w_out": normal_values(arg_keys[7], (H * DH, C), (H * DH) ** -0.5, 0.5),
        "valid_length": jax.random.randint(arg_keys[8], (1,), N // 2, N + 1).astype(jnp.int32),
    }


epsilon = 1e-05

def normalize(pair_rows, ln_gain):
    widened = pair_rows.astype(jnp.float32)
    average = lax.optimization_barrier(jnp.mean(widened, -1, keepdims=True))
    centred = widened - average
    spread = lax.optimization_barrier(jnp.mean(centred * centred, -1, keepdims=True))
    return (centred * lax.rsqrt(spread + epsilon) * ln_gain).astype(jnp.bfloat16)

def reference(pair, ln_gain, w_query, w_key, w_value, w_gate, w_bias, w_out, valid_length):
    length = valid_length[0]
    query_scale = DH ** (-0.5)
    positions = jnp.arange(N, dtype=jnp.int32)
    key_valid = positions < length

    def bias_row(pair_row):
        normed = normalize(pair_row, ln_gain)
        return jnp.dot(normed, w_bias, preferred_element_type=jnp.float32).astype(jnp.bfloat16)
    bias_all = lax.map(bias_row, pair)
    bias_heads = jnp.transpose(bias_all, (2, 0, 1)).astype(jnp.float32)

    def attend_row(inputs):
        pair_row, row_index = inputs
        normed = normalize(pair_row, ln_gain)
        query = (jnp.dot(normed, w_query, preferred_element_type=jnp.float32) * query_scale).astype(jnp.bfloat16)
        key_proj = jnp.dot(normed, w_key, preferred_element_type=jnp.float32).astype(jnp.bfloat16)
        value_proj = jnp.dot(normed, w_value, preferred_element_type=jnp.float32).astype(jnp.bfloat16)
        gating = jax.nn.sigmoid(jnp.dot(normed, w_gate, preferred_element_type=jnp.float32)).astype(jnp.bfloat16)
        query_heads = query.reshape(N, H, DH).astype(jnp.float32)
        key_heads = key_proj.reshape(N, H, DH).astype(jnp.float32)
        value_heads = value_proj.reshape(N, H, DH).astype(jnp.float32)
        scores = jnp.einsum('jhd,khd->hjk', query_heads, key_heads) + bias_heads
        scores = jnp.where(key_valid[None, None, :], scores, -1e+30)
        highest = lax.optimization_barrier(jnp.max(scores, -1, keepdims=True))
        exponent = jnp.exp(scores - highest)
        totals = lax.optimization_barrier(jnp.sum(exponent, -1))
        weights = exponent.astype(jnp.bfloat16).astype(jnp.float32)
        blended = jnp.einsum('hjk,khd->jhd', weights, value_heads) / jnp.transpose(totals)[:, :, None]
        gated = (gating.astype(jnp.float32) * blended.reshape(N, H * DH)).astype(jnp.bfloat16)
        update = jnp.dot(gated, w_out, preferred_element_type=jnp.float32)
        inside = (row_index < length) & key_valid
        return jnp.where(inside[:, None], update, 0.0).astype(jnp.bfloat16)
    return lax.map(attend_row, (pair, positions))
```

```python
import functools

import jax
import jax.numpy as jnp
from jax import lax
from jax.experimental import pallas as pl
from jax.experimental.pallas import tpu as pltpu
from jax.sharding import PartitionSpec as P

epsilon = 1e-05
CHUNKS = 3


def normalize(pair_rows, ln_gain):
    widened = pair_rows.astype(jnp.float32)
    average = jnp.mean(widened, -1, keepdims=True)
    centred = widened - average
    spread = jnp.mean(centred * centred, -1, keepdims=True)
    return (centred * lax.rsqrt(spread + epsilon) * ln_gain).astype(jnp.bfloat16)


def attend(heads, block, normed_ref, bias_ref, merged_ref, out_w_ref, update_ref):
    across, _, tile_cols, channels = normed_ref.shape
    columns, width = across * tile_cols, out_w_ref.shape[0]
    head_size = width // heads
    normed = normed_ref[...].reshape(columns, channels)
    scale = head_size ** (-0.5)

    def project(part):
        weight = merged_ref[:, part * width : (part + 1) * width]
        return jnp.dot(normed, weight, preferred_element_type=jnp.float32)

    query = (project(0) * scale).astype(jnp.bfloat16)
    key_proj = project(1).astype(jnp.bfloat16)
    value_proj = project(2).astype(jnp.bfloat16)
    gating = jax.nn.sigmoid(project(3)).astype(jnp.bfloat16).astype(jnp.float32)
    summed = jnp.concatenate([value_proj, jnp.ones_like(value_proj)], axis=1)
    lane_head = lax.broadcasted_iota(jnp.int32, (block, width), 1) // head_size
    updates = []
    for start in range(0, columns, block):
        span = slice(start, start + block)
        blended = jnp.zeros((block, width), jnp.float32)
        for head in range(heads):
            mine = lane_head == head
            picked = jnp.where(mine, query[span], jnp.zeros((), jnp.bfloat16))
            scores = lax.dot_general(
                picked, key_proj, (((1,), (1,)), ((), ())), preferred_element_type=jnp.float32
            )
            scores = scores + bias_ref[head, span, :].astype(jnp.float32)
            highest = jnp.max(scores, -1, keepdims=True)
            weights = jnp.exp(scores - highest).astype(jnp.bfloat16)
            both = jnp.dot(weights, summed, preferred_element_type=jnp.float32)
            blended = jnp.where(mine, both[:, :width] / both[:, width:], blended)
        gated = (gating[span] * blended).astype(jnp.bfloat16)
        update = jnp.dot(gated, out_w_ref[...], preferred_element_type=jnp.float32)
        updates.append(update.astype(jnp.bfloat16))
    update_ref[...] = jnp.concatenate(updates, axis=0).reshape(update_ref.shape)


def block_of(columns):
    for block in (256, 128, 64, 32, 16):
        if columns % block == 0:
            return block
    return columns


def attention(normed_rows, bias, merged, w_out):
    across, rows, tile_cols, channels = normed_rows.shape
    columns = across * tile_cols
    piece = pl.BlockSpec((across, 1, tile_cols, channels), lambda i: (0, i, 0, 0))
    heads, width = bias.shape[0], w_out.shape[0]
    whole = lambda i: (0, 0)
    cells = rows * heads * columns * columns
    return pl.pallas_call(
        functools.partial(attend, heads, block_of(columns)),
        grid=(rows,),
        in_specs=[
            piece,
            pl.BlockSpec(bias.shape, lambda i: (0, 0, 0)),
            pl.BlockSpec(merged.shape, whole),
            pl.BlockSpec(w_out.shape, whole),
        ],
        out_specs=piece,
        out_shape=jax.ShapeDtypeStruct(normed_rows.shape, jnp.bfloat16),
        compiler_params=pltpu.CompilerParams(vmem_limit_bytes=48 * 1024 * 1024),
        cost_estimate=pl.CostEstimate(
            flops=cells * 768, bytes_accessed=8 * cells // columns * 64, transcendentals=cells
        ),
    )(normed_rows, bias, merged, w_out)


def per_device(pair, ln_gain, w_query, w_key, w_value, w_gate, w_bias, w_out, valid_length):
    tile_rows, tile_cols, channels = pair.shape
    across = lax.axis_size("col")
    own_rows = tile_rows // across
    length = valid_length[0]
    row_at = lax.axis_index("row") * tile_rows + jnp.arange(tile_rows, dtype=jnp.int32)
    col_at = lax.axis_index("col") * tile_cols + jnp.arange(tile_cols, dtype=jnp.int32)
    normed = normalize(pair, ln_gain)
    bias_tile = jnp.einsum(
        "abc,ch->hab", normed, w_bias, preferred_element_type=jnp.float32
    )
    bias_tile = jnp.where(col_at < length, bias_tile, -1e30).astype(jnp.bfloat16)
    merged = jnp.concatenate([w_query, w_key, w_value, w_gate], axis=1)
    bias_cols = lax.all_gather(bias_tile, "col", axis=2, tiled=True)
    bias = lax.all_gather(bias_cols, "row", axis=1, tiled=True)
    step = own_rows // CHUNKS if own_rows % CHUNKS == 0 else own_rows
    tiles = normed.reshape(across, own_rows, tile_cols, channels)
    pieces = []
    for first in range(0, own_rows, step):
        part = lax.all_to_all(tiles[:, first : first + step], "col", split_axis=0, concat_axis=0)
        update = attention(part, bias, merged, w_out)
        pieces.append(lax.all_to_all(update, "col", split_axis=0, concat_axis=0))
    update = jnp.concatenate(pieces, axis=1).reshape(tile_rows, tile_cols, channels)
    inside = (row_at < length)[:, None] & (col_at < length)[None, :]
    return jnp.where(inside[..., None], update, jnp.zeros((), jnp.bfloat16))


def solution(mesh):
    placed = (P("row", "col", None), P(), P(), P(), P(), P(), P(), P(), P())
    return jax.shard_map(
        per_device, mesh=mesh, in_specs=placed, out_specs=P("row", "col", None), check_vma=False
    )
```

```python
import functools

import jax
import jax.numpy as jnp
from jax import lax
from jax.experimental import pallas as pl
from jax.experimental.pallas import tpu as pltpu
from jax.sharding import PartitionSpec as P

epsilon = 1e-05
CHUNKS = 2


def prepare(pair_ref, gain_ref, bias_w_ref, normed_ref, bias_ref):
    widened = pair_ref[...].astype(jnp.float32)
    average = jnp.mean(widened, -1, keepdims=True)
    centred = widened - average
    spread = jnp.mean(centred * centred, -1, keepdims=True)
    normed = (centred * lax.rsqrt(spread + epsilon) * gain_ref[...]).astype(jnp.bfloat16)
    normed_ref[...] = normed
    bias_ref[...] = lax.dot_general(
        bias_w_ref[...], normed, (((1,), (1,)), ((), ())), preferred_element_type=jnp.float32
    )


def normalize(pair, ln_gain, w_bias):
    tile_rows, tile_cols, channels = pair.shape
    cells, heads = tile_rows * tile_cols, w_bias.shape[1]
    block = next(n for n in (2304, 768, 256, 128, cells) if cells % n == 0)
    normed, bias = pl.pallas_call(
        prepare,
        grid=(cells // block,),
        in_specs=[
            pl.BlockSpec((block, channels), lambda i: (i, 0)),
            pl.BlockSpec((1, channels), lambda i: (0, 0)),
            pl.BlockSpec((heads, channels), lambda i: (0, 0)),
        ],
        out_specs=[
            pl.BlockSpec((block, channels), lambda i: (i, 0)),
            pl.BlockSpec((heads, block), lambda i: (0, i)),
        ],
        out_shape=[
            jax.ShapeDtypeStruct((cells, channels), jnp.bfloat16),
            jax.ShapeDtypeStruct((heads, cells), jnp.float32),
        ],
        compiler_params=pltpu.CompilerParams(vmem_limit_bytes=32 * 1024 * 1024),
    )(pair.reshape(cells, channels), ln_gain.reshape(1, channels), w_bias.T)
    return normed, bias.reshape(heads, tile_rows, tile_cols)


def attend(heads, block, limits_ref, normed_ref, bias_ref, merged_ref, out_w_ref, update_ref):
    across, _, tile_cols, channels = normed_ref.shape
    columns, width = across * tile_cols, out_w_ref.shape[0]
    head_size = width // heads
    normed = normed_ref[...].reshape(columns, channels)
    scale = head_size ** (-0.5)

    def project(part):
        weight = merged_ref[:, part * width : (part + 1) * width]
        return jnp.dot(normed, weight, preferred_element_type=jnp.float32)

    query = (project(0) * scale).astype(jnp.bfloat16)
    key_proj = project(1).astype(jnp.bfloat16)
    value_proj = project(2).astype(jnp.bfloat16)
    gating = jax.nn.sigmoid(project(3)).astype(jnp.bfloat16).astype(jnp.float32)
    summed = jnp.concatenate([value_proj, jnp.ones_like(value_proj)], axis=1)
    lane_head = lax.broadcasted_iota(jnp.int32, (block, width), 1) // head_size
    length, first_row = limits_ref[0], limits_ref[1]
    limit = jnp.where(first_row + pl.program_id(0) < length, length, 0)
    place = lax.broadcasted_iota(jnp.int32, (block, channels), 0)
    updates = []
    for start in range(0, columns, block):
        span = slice(start, start + block)
        blended = jnp.zeros((block, width), jnp.float32)
        for head in range(heads):
            mine = lane_head == head
            picked = jnp.where(mine, query[span], jnp.zeros((), jnp.bfloat16))
            scores = lax.dot_general(
                picked, key_proj, (((1,), (1,)), ((), ())), preferred_element_type=jnp.float32
            )
            scores = scores + bias_ref[head, span, :].astype(jnp.float32)
            highest = jnp.max(scores, -1, keepdims=True)
            weights = jnp.exp(scores - highest).astype(jnp.bfloat16)
            both = jnp.dot(weights, summed, preferred_element_type=jnp.float32)
            blended = jnp.where(mine, both[:, :width] / both[:, width:], blended)
        gated = (gating[span] * blended).astype(jnp.bfloat16)
        update = jnp.dot(gated, out_w_ref[...], preferred_element_type=jnp.float32)
        update = jnp.where(place + start < limit, update, 0.0)
        updates.append(update.astype(jnp.bfloat16))
    update_ref[...] = jnp.concatenate(updates, axis=0).reshape(update_ref.shape)


def block_of(columns):
    for block in (256, 128, 64, 32, 16):
        if columns % block == 0:
            return block
    return columns


def attention(limits, normed_rows, bias, merged, w_out):
    across, rows, tile_cols, channels = normed_rows.shape
    columns = across * tile_cols
    piece = pl.BlockSpec((across, 1, tile_cols, channels), lambda i: (0, i, 0, 0))
    heads, width = bias.shape[0], w_out.shape[0]
    whole = lambda i: (0, 0)
    cells = rows * heads * columns * columns
    return pl.pallas_call(
        functools.partial(attend, heads, block_of(columns)),
        grid=(rows,),
        in_specs=[
            pl.BlockSpec(memory_space=pltpu.SMEM),
            piece,
            pl.BlockSpec(bias.shape, lambda i: (0, 0, 0)),
            pl.BlockSpec(merged.shape, whole),
            pl.BlockSpec(w_out.shape, whole),
        ],
        out_specs=piece,
        out_shape=jax.ShapeDtypeStruct(normed_rows.shape, jnp.bfloat16),
        compiler_params=pltpu.CompilerParams(vmem_limit_bytes=48 * 1024 * 1024),
        cost_estimate=pl.CostEstimate(
            flops=cells * 768, bytes_accessed=8 * cells // columns * 64, transcendentals=cells
        ),
    )(limits, normed_rows, bias, merged, w_out)


def per_device(pair, ln_gain, w_query, w_key, w_value, w_gate, w_bias, w_out, valid_length):
    tile_rows, tile_cols, channels = pair.shape
    across = lax.axis_size("col")
    own_rows = tile_rows // across
    length = valid_length[0]
    first_own = lax.axis_index("row") * tile_rows + lax.axis_index("col") * own_rows
    col_at = lax.axis_index("col") * tile_cols + jnp.arange(tile_cols, dtype=jnp.int32)
    normed, bias_tile = normalize(pair, ln_gain, w_bias)
    bias_tile = jnp.where(col_at < length, bias_tile, -1e30).astype(jnp.bfloat16)
    merged = jnp.concatenate([w_query, w_key, w_value, w_gate], axis=1)
    heads = bias_tile.shape[0]
    repeated = jnp.broadcast_to(bias_tile.reshape(1, -1, channels), (across, bias_tile.size // channels, channels))
    bias_cols = lax.all_to_all(repeated, "col", split_axis=0, concat_axis=0)
    bias_cols = bias_cols.reshape(across, heads, tile_rows, tile_cols)
    bias_cols = jnp.moveaxis(bias_cols, 0, 2).reshape(heads, tile_rows, across * tile_cols)
    bias = lax.all_gather(bias_cols, "row", axis=1, tiled=True)
    step = own_rows // CHUNKS if own_rows % CHUNKS == 0 else own_rows
    tiles = normed.reshape(across, own_rows, tile_cols, channels)
    pieces = []
    for first in range(0, own_rows, step):
        part = lax.all_to_all(tiles[:, first : first + step], "col", split_axis=0, concat_axis=0)
        limits = jnp.stack([length, first_own + first])
        update = attention(limits, part, bias, merged, w_out)
        pieces.append(lax.all_to_all(update, "col", split_axis=0, concat_axis=0))
    return jnp.concatenate(pieces, axis=1).reshape(tile_rows, tile_cols, channels)


def solution(mesh):
    placed = (P("row", "col", None), P(), P(), P(), P(), P(), P(), P(), P())
    return jax.shard_map(
        per_device, mesh=mesh, in_specs=placed, out_specs=P("row", "col", None), check_vma=False
    )
```

```python
import functools

import jax
import jax.numpy as jnp
from jax import lax
from jax.experimental import pallas as pl
from jax.experimental.pallas import tpu as pltpu
from jax.sharding import PartitionSpec as P

epsilon = 1e-05
CHUNKS = 2


def prepare(pair_ref, gain_ref, bias_w_ref, normed_ref, bias_ref):
    widened = pair_ref[...].astype(jnp.float32)
    average = jnp.mean(widened, -1, keepdims=True)
    centred = widened - average
    spread = jnp.mean(centred * centred, -1, keepdims=True)
    normed = (centred * lax.rsqrt(spread + epsilon) * gain_ref[...]).astype(jnp.bfloat16)
    normed_ref[...] = normed
    bias_ref[...] = lax.dot_general(
        bias_w_ref[...], normed, (((1,), (1,)), ((), ())), preferred_element_type=jnp.float32
    )


def normalize(pair, ln_gain, w_bias):
    tile_rows, tile_cols, channels = pair.shape
    cells, heads = tile_rows * tile_cols, w_bias.shape[1]
    block = next(n for n in (2304, 768, 256, 128, cells) if cells % n == 0)
    normed, bias = pl.pallas_call(
        prepare,
        grid=(cells // block,),
        in_specs=[
            pl.BlockSpec((block, channels), lambda i: (i, 0)),
            pl.BlockSpec((1, channels), lambda i: (0, 0)),
            pl.BlockSpec((heads, channels), lambda i: (0, 0)),
        ],
        out_specs=[
            pl.BlockSpec((block, channels), lambda i: (i, 0)),
            pl.BlockSpec((heads, block), lambda i: (0, i)),
        ],
        out_shape=[
            jax.ShapeDtypeStruct((cells, channels), jnp.bfloat16),
            jax.ShapeDtypeStruct((heads, cells), jnp.float32),
        ],
        compiler_params=pltpu.CompilerParams(vmem_limit_bytes=32 * 1024 * 1024),
    )(pair.reshape(cells, channels), ln_gain.reshape(1, channels), w_bias.T)
    return normed, bias.reshape(heads, tile_rows, tile_cols)


def attend(heads, block, limits_ref, normed_ref, bias_ref, merged_ref, out_w_ref, update_ref):
    across, _, tile_cols, channels = normed_ref.shape
    columns, width = across * tile_cols, out_w_ref.shape[0]
    head_size = width // heads
    normed = normed_ref[...].reshape(columns, channels)
    scale = head_size ** (-0.5)

    def project(part):
        weight = merged_ref[:, part * width : (part + 1) * width]
        return jnp.dot(normed, weight, preferred_element_type=jnp.float32)

    query = (project(0) * scale).astype(jnp.bfloat16)
    key_proj = project(1).astype(jnp.bfloat16)
    value_proj = project(2).astype(jnp.bfloat16)
    gating = jax.nn.sigmoid(project(3)).astype(jnp.bfloat16).astype(jnp.float32)
    summed = jnp.concatenate([value_proj, jnp.ones_like(value_proj)], axis=1)
    lane_head = lax.broadcasted_iota(jnp.int32, (block, width), 1) // head_size
    length, first_row = limits_ref[0], limits_ref[1]
    limit = jnp.where(first_row + pl.program_id(0) < length, length, 0)
    place = lax.broadcasted_iota(jnp.int32, (block, channels), 0)
    updates = []
    for start in range(0, columns, block):
        span = slice(start, start + block)
        blended = jnp.zeros((block, width), jnp.float32)
        for head in range(heads):
            mine = lane_head == head
            picked = jnp.where(mine, query[span], jnp.zeros((), jnp.bfloat16))
            scores = lax.dot_general(
                picked, key_proj, (((1,), (1,)), ((), ())), preferred_element_type=jnp.float32
            )
            scores = scores + bias_ref[head, span, :].astype(jnp.float32)
            highest = jnp.max(scores, -1, keepdims=True)
            weights = jnp.exp(scores - highest).astype(jnp.bfloat16)
            both = jnp.dot(weights, summed, preferred_element_type=jnp.float32)
            blended = jnp.where(mine, both[:, :width] / both[:, width:], blended)
        gated = (gating[span] * blended).astype(jnp.bfloat16)
        update = jnp.dot(gated, out_w_ref[...], preferred_element_type=jnp.float32)
        update = jnp.where(place + start < limit, update, 0.0)
        updates.append(update.astype(jnp.bfloat16))
    update_ref[...] = jnp.concatenate(updates, axis=0).reshape(update_ref.shape)


def block_of(columns):
    for block in (384, 256, 128, 64, 32, 16):
        if columns % block == 0:
            return block
    return columns


def attention(limits, normed_rows, bias, merged, w_out):
    across, rows, tile_cols, channels = normed_rows.shape
    columns = across * tile_cols
    piece = pl.BlockSpec((across, 1, tile_cols, channels), lambda i: (0, i, 0, 0))
    heads, width = bias.shape[0], w_out.shape[0]
    whole = lambda i: (0, 0)
    cells = rows * heads * columns * columns
    return pl.pallas_call(
        functools.partial(attend, heads, block_of(columns)),
        grid=(rows,),
        in_specs=[
            pl.BlockSpec(memory_space=pltpu.SMEM),
            piece,
            pl.BlockSpec(bias.shape, lambda i: (0, 0, 0)),
            pl.BlockSpec(merged.shape, whole),
            pl.BlockSpec(w_out.shape, whole),
        ],
        out_specs=piece,
        out_shape=jax.ShapeDtypeStruct(normed_rows.shape, jnp.bfloat16),
        compiler_params=pltpu.CompilerParams(vmem_limit_bytes=48 * 1024 * 1024),
        cost_estimate=pl.CostEstimate(
            flops=cells * 768, bytes_accessed=8 * cells // columns * 64, transcendentals=cells
        ),
    )(limits, normed_rows, bias, merged, w_out)


def per_device(pair, ln_gain, w_query, w_key, w_value, w_gate, w_bias, w_out, valid_length):
    tile_rows, tile_cols, channels = pair.shape
    across = lax.axis_size("col")
    own_rows = tile_rows // across
    length = valid_length[0]
    first_own = lax.axis_index("row") * tile_rows + lax.axis_index("col") * own_rows
    col_at = lax.axis_index("col") * tile_cols + jnp.arange(tile_cols, dtype=jnp.int32)
    normed, bias_tile = normalize(pair, ln_gain, w_bias)
    bias_tile = jnp.where(col_at < length, bias_tile, -1e30).astype(jnp.bfloat16)
    merged = jnp.concatenate([w_query, w_key, w_value, w_gate], axis=1)
    heads = bias_tile.shape[0]
    repeated = jnp.broadcast_to(bias_tile.reshape(1, -1, channels), (across, bias_tile.size // channels, channels))
    bias_cols = lax.all_to_all(repeated, "col", split_axis=0, concat_axis=0)
    bias_cols = bias_cols.reshape(across, heads, tile_rows, tile_cols)
    bias_cols = jnp.moveaxis(bias_cols, 0, 2).reshape(heads, tile_rows, across * tile_cols)
    bias = lax.all_gather(bias_cols, "row", axis=1, tiled=True)
    step = own_rows // CHUNKS if own_rows % CHUNKS == 0 else own_rows
    tiles = normed.reshape(across, own_rows, tile_cols, channels)
    pieces = []
    for first in range(0, own_rows, step):
        part = lax.all_to_all(tiles[:, first : first + step], "col", split_axis=0, concat_axis=0)
        limits = jnp.stack([length, first_own + first])
        update = attention(limits, part, bias, merged, w_out)
        pieces.append(lax.all_to_all(update, "col", split_axis=0, concat_axis=0))
    return jnp.concatenate(pieces, axis=1).reshape(tile_rows, tile_cols, channels)


def solution(mesh):
    placed = (P("row", "col", None), P(), P(), P(), P(), P(), P(), P(), P())
    return jax.shard_map(
        per_device, mesh=mesh, in_specs=placed, out_specs=P("row", "col", None), check_vma=False
    )
```
